32 devices in a mesh: inst: 4 (over y, x), cell: 8 (over z, core).
Axes of the slice: x: 2, y: 2, z: 4, core: 2. Of those that a mesh axis runs over, the one named last changes fastest.
Arguments:
- adjoint_init: float32 [8, 24, 8, 320], P('inst', 'cell'), may hold values from -6 to 6
- source_term: float32 [8, 24, 8, 320], P('inst', 'cell'), may hold values from -6 to 6
- jacobian: bfloat16 [8, 24, 3, 320, 320], P('inst', 'cell')
- volume: float32 [24, 320], P('cell'), may hold values from 0.5 to 2
- pseudo_step: float32 [24, 320], P('cell'), may hold values from 0.2 to 0.6
- neighbor_slots: int32 [24, 3], P('cell'), may hold values from 0 to 6, as said below
- halo_blocks: int32 [32], P('cell'), may hold values from 0 to 2, as said below
- padded_rows: int32 [8], P('cell'), may hold values from 0 to 1
Outputs:
- adjoint: float32 [8, 24, 8, 320], P('inst', 'cell')
- residual: float32 [8, 24, 8, 320], P('inst', 'cell')
The draws below stay inside these ranges and needn't reach their ends.
Inputs may be any that keep to these rules, and one draw needn't show every extreme that they name: `neighbor_slots`: slot 0 of block row r is its own block, 2 + (r mod 3); slot 1 is below 2; slot 2 is 5 or more. `halo_blocks`: each device's 2 * 2 entries are its local block rows, the first 2 for the previous device, the others for the next; every entry is below 3 minus that device's padded rows.
All inputs are finite; a program needn't handle non-finite values.
Results may differ from the reference program's by a relative error of at most 0.0003.
Values sent between devices are 32-bit elements; how exact they have to be, the bound alone decides.
A program may use at most 64 MiB of HBM per device.

```python
import math
import jax
import jax.numpy as jnp
from jax import lax

NT = 8
BS = 320
K = 3
HL = 2
PADMAX = 1
RB = 3
NOBJ = 8
ITERS = 16
BLOCKS = 24


def shared_pads(key):
    ncell = BLOCKS // RB
    pad_key = jax.random.fold_in(key, 101)
    counts = jax.random.randint(pad_key, (ncell,), 0, PADMAX + 1)
    counts = counts.at[0].set(PADMAX)
    counts = counts.at[1].set(0)
    return counts.astype(jnp.int32)


def draw_padded_rows(key, part):
    return shared_pads(key)


def draw_halo_blocks(key, part):
    ncell = BLOCKS // RB
    counts = shared_pads(key)
    key = jax.random.fold_in(key, 2)
    livecount = (RB - counts)[:, None]
    entries = jax.random.randint(key, (ncell, 2 * HL), 0, livecount)
    entries = entries.at[1, 0].set(0)
    entries = entries.at[1, 2 * HL - 1].set(RB - 1)
    return entries.reshape(-1).astype(jnp.int32)


def draw_neighbor_slots(key, part):
    key = jax.random.fold_in(key, 3)
    first_key, second_key = jax.random.split(key)
    rows = jnp.arange(BLOCKS, dtype=jnp.int32)
    own_slot = HL + jnp.remainder(rows, RB)
    prev_slot = jax.random.randint(first_key, (BLOCKS,), 0, HL)
    next_slot = HL + RB + jax.random.randint(second_key, (BLOCKS,), 0, HL)
    return jnp.stack([own_slot, prev_slot, next_slot], axis=1).astype(jnp.int32)


def draw_jacobian(key, part):
    key = jax.random.fold_in(key, 4)
    shape = (NT, BLOCKS, K, BS, BS)
    noise = jax.random.normal(key, shape, jnp.float32)
    noise = noise * (0.3 / BS ** 0.5)
    eye = (jnp.arange(BS)[:, None] == jnp.arange(BS)[None, :]).astype(jnp.float32)
    first = (jnp.arange(K) == 0).astype(jnp.float32)[:, None, None]
    blocks = noise + (first * eye)[None, None]
    return blocks.astype(jnp.bfloat16)


def shard_levels(key, dims, shards, smallest, largest):
    def one(position, shards_of):
        steps = jax.random.uniform(jax.random.fold_in(jax.random.fold_in(key, 6), position), (shards_of,), jnp.float32, smallest / len(shards), largest / len(shards))
        return jnp.repeat(jnp.exp(steps), dims[position] // shards_of).reshape((-1,) + (1,) * (len(dims) - position - 1))

    loudness = one(*shards[0])
    for cut in shards[1:]:
        loudness = loudness * one(*cut)
    return loudness


def scatter_about(stream_key, extent, deviation, reach, cuts=(), held_as=jnp.bfloat16):
    loudness = shard_levels(stream_key, extent, cuts, -0.22, 0.18) if cuts else 1.0
    array = jax.random.normal(stream_key, extent, jnp.float32) * deviation * loudness
    return jnp.minimum(jnp.maximum(array, -reach), reach).astype(held_as)


def setup_inputs(seed: int = 0) -> dict:
    splits = jax.random.split(jax.random.key(seed), 9)
    adjoint_init = scatter_about(splits[0], (NT, BLOCKS, NOBJ, BS), 1.0, 6.0, ((0, 4), (1, 8)), jnp.float32)
    source_term = scatter_about(splits[1], (NT, BLOCKS, NOBJ, BS), 1.0, 6.0, ((0, 4), (1, 8)), jnp.float32)
    jacobian = draw_jacobian(jax.random.fold_in(splits[8], 71), 0)
    volume = jnp.clip(jnp.exp(math.log(2.0) - 1.3862944 * jax.random.uniform(splits[3], (BLOCKS, BS), jnp.float32) ** shard_levels(splits[3], (BLOCKS, BS), ((0, 8),), -0.2, 0.2)), 0.5, 2.0)
    pseudo_step = jnp.clip(jnp.exp(math.log(0.6) - 1.0986123 * jax.random.uniform(splits[4], (BLOCKS, BS), jnp.float32) ** shard_levels(splits[4], (BLOCKS, BS), ((0, 8),), -0.2, 0.2)), 0.2, 0.6)
    neighbor_slots = draw_neighbor_slots(jax.random.fold_in(splits[8], 71), 0)
    halo_blocks = draw_halo_blocks(jax.random.fold_in(splits[8], 71), 0)
    padded_rows = draw_padded_rows(jax.random.fold_in(splits[8], 71), 0)
    return {"adjoint_init": adjoint_init, "source_term": source_term, "jacobian": jacobian, "volume": volume, "pseudo_step": pseudo_step, "neighbor_slots": neighbor_slots, "halo_blocks": halo_blocks, "padded_rows": padded_rows}


spectral_scale = 0.15


def time_matrix():
    idx = jnp.arange(NT, dtype=jnp.int32)
    diff = idx[:, None] - idx[None, :]
    parity = jnp.where(jnp.remainder(diff, 2) == 0, 1.0, -1.0).astype(jnp.float32)
    angle = jnp.float32(math.pi) * diff.astype(jnp.float32) / NT
    sine = jnp.where(diff == 0, jnp.float32(1.0), jnp.sin(angle))
    return jnp.where(diff == 0, jnp.float32(0.0), 0.5 * parity * jnp.cos(angle) / sine).astype(jnp.float32)


def reference(adjoint_init, source_term, jacobian, volume, pseudo_step, neighbor_slots, halo_blocks, padded_rows):
    ncell = BLOCKS // RB
    rows = jnp.arange(BLOCKS, dtype=jnp.int32)
    device = rows // RB
    before = jnp.remainder(device - 1, ncell).astype(jnp.int32)
    after = jnp.remainder(device + 1, ncell).astype(jnp.int32)
    lists = halo_blocks.reshape(ncell, 2 * HL)
    codes = neighbor_slots
    own_block = device[:, None] * RB + codes - HL
    pick_prev = jnp.take_along_axis(lists[before], HL + jnp.clip(codes, 0, HL - 1), axis=1)
    pick_next = jnp.take_along_axis(lists[after], jnp.clip(codes - HL - RB, 0, HL - 1), axis=1)
    from_prev = before[:, None] * RB + pick_prev
    from_next = after[:, None] * RB + pick_next
    column = jnp.where(codes < HL, from_prev, jnp.where(codes < HL + RB, own_block, from_next)).astype(jnp.int32)
    live = (jnp.remainder(rows, RB) < RB - padded_rows[device]).astype(jnp.float32)[None, :, None, None]
    weights = time_matrix()
    scale = (spectral_scale * volume)[None, :, None, :]
    step_size = pseudo_step[None, :, None, :]

    def per_instance(pair):
        plane, blocks = pair
        gathered = plane[column]
        return jnp.einsum('rkop,rkpq->roq', gathered, blocks.astype(jnp.float32), precision=lax.Precision.HIGHEST)

    adjoint = adjoint_init
    residual = jnp.zeros_like(adjoint_init)
    for sweep in range(ITERS):
        flux = lax.map(per_instance, (adjoint, jacobian))
        coupled = jnp.einsum('ji,jroq->iroq', weights, adjoint, precision=lax.Precision.HIGHEST)
        residual = live * (source_term - flux - scale * coupled)
        adjoint = adjoint + step_size * residual
    return adjoint, residual
```

```python
import functools
import math

import jax
import jax.numpy as jnp
from jax import lax
from jax.experimental import pallas as pl
from jax.experimental.pallas import tpu as pltpu
from jax.sharding import PartitionSpec as P

ITERS = 16
TERMS = 2
MESH = pl.DeviceIdType.MESH

spectral_scale = 0.15


def time_weight(diff, count):
    diff = diff % count
    if diff == 0:
        return 0.0
    angle = math.pi * diff / count
    return 0.5 * (-1.0) ** diff * math.cos(angle) / math.sin(angle)


def kernel(
    insts,
    cells,
    slots_ref,
    halo_ref,
    pad_ref,
    init_ref,
    src_in_ref,
    jac_ref,
    vol_ref,
    step_in_ref,
    adj_out,
    res_out,
    adj,
    halo_out,
    from_prev,
    from_next,
    peers,
    src,
    step,
    scale,
    near,
    far,
    prev_parts,
    next_parts,
    flux,
    send_sem,
    prev_sem,
    next_sem,
    peer_sem,
):
    rows, width = vol_ref.shape
    reach = from_prev.shape[1]
    objectives = adj.shape[2]
    packed = adj.shape[3]
    main = width // 128 * 128
    tail = width - main
    wide = main + 128
    a = lax.axis_index("inst")
    d = lax.axis_index("cell")
    before = lax.rem(d + cells - 1, cells)
    after = lax.rem(d + 1, cells)
    others = [lax.rem(a + m, insts) for m in range(1, insts)]

    barrier = pltpu.get_barrier_semaphore()
    for c in (before, after):
        pl.semaphore_signal(barrier, inc=1, device_id={"cell": c}, device_id_type=MESH)
    for b in others:
        pl.semaphore_signal(barrier, inc=1, device_id={"inst": b}, device_id_type=MESH)

    def pack(first, second):
        return jnp.concatenate(
            [first[:, :main], first[:, main:], second[:, main:], second[:, :main]], axis=1
        )

    for r in range(rows):
        adj[0, r] = pack(init_ref[0, r], init_ref[1, r])
        src[r] = pack(src_in_ref[0, r], src_in_ref[1, r])
        v = jnp.broadcast_to(vol_ref[r : r + 1, :], (objectives, width)) * spectral_scale
        scale[r] = pack(v, v)
        v = jnp.broadcast_to(step_in_ref[r : r + 1, :], (objectives, width))
        step[r] = pack(v, v)

    def expand(t, r, k, dst):
        block = jac_ref.at[t, r, k]
        if t == 0:
            dst[:width, :main] = block[:, :main]
            dst[:width, main:] = jnp.concatenate(
                [block[:, main:], jnp.zeros((width, 128 - tail), jnp.bfloat16)], axis=1
            )
            dst[width:, :] = jnp.zeros((wide - width, wide), jnp.bfloat16)
        else:
            for lo, hi, at in ((0, main, 128), (main, width, 128 - tail)):
                dst[at : at + hi - lo, 128:] = block[lo:hi, :main]
                dst[at : at + hi - lo, :128] = jnp.concatenate(
                    [jnp.zeros((hi - lo, 128 - tail), jnp.bfloat16), block[lo:hi, main:]], axis=1
                )
            dst[: 128 - tail, :] = jnp.zeros((128 - tail, wide), jnp.bfloat16)

    for r in range(rows):
        for t in range(2):
            expand(t, r, 0, near.at[r, t])
            for k in (1, 2):
                expand(t, r, k, far.at[r, t, (k - 1) * wide : k * wide, :])

    def split(x):
        parts = []
        for _ in range(TERMS):
            high = x.astype(jnp.bfloat16).astype(jnp.float32)
            parts.append(high)
            x = x - high
        return jnp.concatenate(parts, axis=0).astype(jnp.bfloat16)

    def join(x):
        total = x[objectives * (TERMS - 1) :]
        for n in reversed(range(TERMS - 1)):
            total = total + x[objectives * n : objectives * (n + 1)]
        return total

    def merge(first, second):
        return jnp.concatenate(
            [first[:, :main], first[:, main:] + second[:, :128], second[:, 128:]], axis=1
        )

    live = [
        jnp.where(r < rows - pad_ref[0], jnp.float32(1), jnp.float32(0)) for r in range(rows)
    ]
    lane = lax.broadcasted_iota(jnp.int32, (objectives, 128), 1)
    first_half = lane < tail

    pl.semaphore_wait(barrier, insts + 1)

    def sweep(s, carry):
        now = lax.rem(s, 2)
        later = 1 - now
        for h in range(2 * reach):
            halo_out[now, h] = adj[now, halo_ref[h]]
        copies = [
            pltpu.make_async_remote_copy(
                halo_out.at[now, 0:reach],
                from_next.at[now],
                send_sem.at[now, 0],
                next_sem.at[now],
                device_id={"cell": before},
                device_id_type=MESH,
            ),
            pltpu.make_async_remote_copy(
                halo_out.at[now, reach : 2 * reach],
                from_prev.at[now],
                send_sem.at[now, 1],
                prev_sem.at[now],
                device_id={"cell": after},
                device_id_type=MESH,
            ),
        ]
        for m in range(1, insts):
            copies.append(
                pltpu.make_async_remote_copy(
                    adj.at[now],
                    peers.at[now, insts - m - 1],
                    send_sem.at[now, 1 + m],
                    peer_sem.at[now, insts - m - 1],
                    device_id={"inst": others[m - 1]},
                    device_id_type=MESH,
                )
            )
        for copy in copies:
            copy.start()

        for r in range(rows):
            x = split(adj[now, r])
            flux[r] = merge(
                join(jnp.dot(x[:, :wide], near[r, 0], preferred_element_type=jnp.float32)),
                join(jnp.dot(x[:, packed - wide :], near[r, 1], preferred_element_type=jnp.float32)),
            )

        copies[0].wait_recv()
        for h in range(reach):
            next_parts[h] = split(from_next[now, h])
        copies[1].wait_recv()
        for h in range(reach):
            prev_parts[h] = split(from_prev[now, h])
        for r in range(rows):
            p = prev_parts[jnp.clip(slots_ref[r, 1], 0, reach - 1)]
            q = next_parts[jnp.clip(slots_ref[r, 2] - reach - rows, 0, reach - 1)]
            flux[r] += merge(
                join(
                    jnp.dot(
                        jnp.concatenate([p[:, :wide], q[:, :wide]], axis=1),
                        far[r, 0],
                        preferred_element_type=jnp.float32,
                    )
                ),
                join(
                    jnp.dot(
                        jnp.concatenate([p[:, packed - wide :], q[:, packed - wide :]], axis=1),
                        far[r, 1],
                        preferred_element_type=jnp.float32,
                    )
                ),
            )

        for copy in copies[2:]:
            copy.wait_recv()
        count = 2 * insts
        for r in range(rows):
            first, middle, second = 0.0, 0.0, 0.0
            cross = 0.0
            for m in range(insts):
                u = adj[now, r] if m == 0 else peers[now, m - 1, r]
                same = time_weight(2 * m, count)
                up = time_weight(2 * m + 1, count)
                down = time_weight(2 * m - 1, count)
                u0, ut, u1 = u[:, :main], u[:, main:wide], u[:, wide:]
                first = first + same * u0 + up * u1
                second = second + same * u1 + down * u0
                middle = middle + same * ut
                cross = cross + jnp.where(first_half, down, up) * ut
            middle = middle + pltpu.roll(cross, tail, 1)
            coupled = jnp.concatenate([first, middle, second], axis=1)
            old = adj[now, r]
            residual = live[r] * (src[r] - flux[r] - scale[r] * coupled)
            new = old + step[r] * residual
            adj[later, r] = new

            @pl.when(s == ITERS - 1)
            def _():
                for out, value in ((adj_out, new), (res_out, residual)):
                    out[0, r, :, :main] = value[:, :main]
                    out[0, r, :, main:] = value[:, main:width]
                    out[1, r, :, :main] = value[:, wide:]
                    out[1, r, :, main:] = value[:, width:wide]

        for copy in copies:
            copy.wait_send()
        return carry

    lax.fori_loop(0, ITERS, sweep, 0)


def on_device(
    insts,
    cells,
    adjoint_init,
    source_term,
    jacobian,
    volume,
    pseudo_step,
    neighbor_slots,
    halo_blocks,
    padded_rows,
):
    inst_local, rows, objectives, width = adjoint_init.shape
    reach = halo_blocks.shape[0] // 2
    main = width // 128 * 128
    wide = main + 128
    packed = inst_local * width
    out = jax.ShapeDtypeStruct(adjoint_init.shape, jnp.float32)
    smem = pl.BlockSpec(memory_space=pltpu.SMEM)
    vmem = pl.BlockSpec(memory_space=pltpu.VMEM)
    f32, bf16 = jnp.float32, jnp.bfloat16
    block = (objectives, packed)
    parts = (objectives * TERMS, packed)
    flops = ITERS * 2 * rows * 3 * inst_local * 16 * width * width
    return pl.pallas_call(
        functools.partial(kernel, insts, cells),
        out_shape=(out, out),
        in_specs=[smem] * 3 + [vmem] * 5,
        out_specs=(vmem, vmem),
        scratch_shapes=[
            pltpu.VMEM((2, rows) + block, f32),
            pltpu.VMEM((2, 2 * reach) + block, f32),
            pltpu.VMEM((2, reach) + block, f32),
            pltpu.VMEM((2, reach) + block, f32),
            pltpu.VMEM((2, insts - 1, rows) + block, f32),
            pltpu.VMEM((rows,) + block, f32),
            pltpu.VMEM((rows,) + block, f32),
            pltpu.VMEM((rows,) + block, f32),
            pltpu.VMEM((rows, 2, wide, wide), bf16),
            pltpu.VMEM((rows, 2, 2 * wide, wide), bf16),
            pltpu.VMEM((reach,) + parts, bf16),
            pltpu.VMEM((reach,) + parts, bf16),
            pltpu.VMEM((rows,) + block, f32),
            pltpu.SemaphoreType.DMA((2, insts + 1)),
            pltpu.SemaphoreType.DMA((2,)),
            pltpu.SemaphoreType.DMA((2,)),
            pltpu.SemaphoreType.DMA((2, insts - 1)),
        ],
        compiler_params=pltpu.CompilerParams(
            collective_id=0, has_side_effects=True, vmem_limit_bytes=40 * 1024 * 1024
        ),
        cost_estimate=pl.CostEstimate(
            flops=flops, bytes_accessed=2 * jacobian.size, transcendentals=0
        ),
        name="relax",
    )(
        neighbor_slots,
        halo_blocks,
        padded_rows,
        adjoint_init,
        source_term,
        jacobian,
        volume,
        pseudo_step,
    )


def solution(mesh):
    return jax.shard_map(
        functools.partial(on_device, mesh.shape["inst"], mesh.shape["cell"]),
        mesh=mesh,
        in_specs=(
            P("inst", "cell", None, None),
            P("inst", "cell", None, None),
            P("inst", "cell", None, None, None),
            P("cell", None),
            P("cell", None),
            P("cell", None),
            P("cell"),
            P("cell"),
        ),
        out_specs=(P("inst", "cell", None, None), P("inst", "cell", None, None)),
        check_vma=False,
    )
```

```python
import functools
import math

import jax
import jax.numpy as jnp
from jax import lax
from jax.experimental import pallas as pl
from jax.experimental.pallas import tpu as pltpu
from jax.sharding import PartitionSpec as P

ITERS = 16
TERMS = 2
MESH = pl.DeviceIdType.MESH

spectral_scale = 0.15


def time_weight(diff, count):
    diff = diff % count
    if diff == 0:
        return 0.0
    angle = math.pi * diff / count
    return 0.5 * (-1.0) ** diff * math.cos(angle) / math.sin(angle)


def kernel(
    insts,
    cells,
    slots_ref,
    halo_ref,
    pad_ref,
    init_hbm,
    src_hbm,
    jac_hbm,
    vol_hbm,
    step_hbm,
    adj_out,
    res_out,
    init_ref,
    src_in_ref,
    jac_ref,
    vol_ref,
    step_in_ref,
    adj,
    halo_out,
    from_prev,
    from_next,
    raw_in,
    part_out,
    part_in,
    src,
    step,
    scale,
    near,
    far,
    prev_parts,
    next_parts,
    flux,
    coupled,
    send_sem,
    prev_sem,
    next_sem,
    raw_sem,
    part_sem,
    load_sem,
):
    rows, width = vol_ref.shape
    assert insts == 4
    reach = from_prev.shape[1]
    objectives = adj.shape[2]
    packed = adj.shape[3]
    main = width // 128 * 128
    tail = width - main
    wide = main + 128
    a = lax.axis_index("inst")
    d = lax.axis_index("cell")
    before = lax.rem(d + cells - 1, cells)
    after = lax.rem(d + 1, cells)
    x_odd = lax.rem(a, 2)
    even = x_odd == 0
    x_peer = a + 1 - 2 * x_odd
    y_peer = lax.rem(a + 2, insts)
    cut = (rows + 1) // 2
    swap = lax.rem(d, 2)
    near_x = swap == 0
    one = x_peer + swap * (y_peer - x_peer)
    two = y_peer + swap * (x_peer - y_peer)
    groups = [(slice(0, cut), one, two, near_x), (slice(cut, rows), two, one, swap == 1)]

    loads = [
        pltpu.make_async_copy(hbm, ref, load_sem.at[n])
        for n, (hbm, ref) in enumerate(
            (
                (init_hbm, init_ref),
                (src_hbm, src_in_ref),
                (vol_hbm, vol_ref),
                (step_hbm, step_in_ref),
                (jac_hbm, jac_ref),
            )
        )
    ]
    for load in loads:
        load.start()

    barrier = pltpu.get_barrier_semaphore()
    for c in (before, after):
        pl.semaphore_signal(barrier, inc=1, device_id={"cell": c}, device_id_type=MESH)
    for b in (x_peer, y_peer):
        pl.semaphore_signal(barrier, inc=1, device_id={"inst": b}, device_id_type=MESH)

    def pack(first, second):
        return jnp.concatenate(
            [first[:, :main], first[:, main:], second[:, main:], second[:, :main]], axis=1
        )

    for load in loads[:4]:
        load.wait()
    for r in range(rows):
        adj[0, r] = pack(init_ref[0, r], init_ref[1, r])
        src[r] = pack(src_in_ref[0, r], src_in_ref[1, r])
        v = jnp.broadcast_to(vol_ref[r : r + 1, :], (objectives, width)) * spectral_scale
        scale[r] = pack(v, v)
        v = jnp.broadcast_to(step_in_ref[r : r + 1, :], (objectives, width))
        step[r] = pack(v, v)

    def expand(t, r, k, dst):
        block = jac_ref.at[t, r, k]
        if t == 0:
            dst[:width, :main] = block[:, :main]
            dst[:width, main:] = jnp.concatenate(
                [block[:, main:], jnp.zeros((width, 128 - tail), jnp.bfloat16)], axis=1
            )
            dst[width:, :] = jnp.zeros((wide - width, wide), jnp.bfloat16)
        else:
            for lo, hi, at in ((0, main, 128), (main, width, 128 - tail)):
                dst[at : at + hi - lo, 128:] = block[lo:hi, :main]
                dst[at : at + hi - lo, :128] = jnp.concatenate(
                    [jnp.zeros((hi - lo, 128 - tail), jnp.bfloat16), block[lo:hi, main:]], axis=1
                )
            dst[: 128 - tail, :] = jnp.zeros((128 - tail, wide), jnp.bfloat16)

    def split(x):
        parts = []
        for _ in range(TERMS):
            high = x.astype(jnp.bfloat16).astype(jnp.float32)
            parts.append(high)
            x = x - high
        return jnp.concatenate(parts, axis=0).astype(jnp.bfloat16)

    def join(x):
        total = x[objectives * (TERMS - 1) :]
        for n in reversed(range(TERMS - 1)):
            total = total + x[objectives * n : objectives * (n + 1)]
        return total

    def merge(first, second):
        return jnp.concatenate(
            [first[:, :main], first[:, main:] + second[:, :128], second[:, 128:]], axis=1
        )

    live = [
        jnp.where(r < rows - pad_ref[0], jnp.float32(1), jnp.float32(0)) for r in range(rows)
    ]
    lane = lax.broadcasted_iota(jnp.int32, (objectives, 128), 1)
    first_half = lane < tail

    pl.semaphore_wait(barrier, 4)

    count = 2 * insts

    def weights(offset):
        return [time_weight(2 * offset + n, count) for n in (0, 1, -1)]

    def choose(flag, first, second):
        return [jnp.where(flag, jnp.float32(p), jnp.float32(q)) for p, q in zip(first, second)]

    ahead = choose(even, weights(1), weights(-1))
    behind = choose(even, weights(-1), weights(1))
    across = weights(2)

    def mix(sources):
        first, middle, second, cross = 0.0, 0.0, 0.0, 0.0
        for u, (same, up, down) in sources:
            u0, ut, u1 = u[:, :main], u[:, main:wide], u[:, wide:]
            first = first + same * u0 + up * u1
            second = second + same * u1 + down * u0
            middle = middle + same * ut
            cross = cross + jnp.where(first_half, down, up) * ut
        return jnp.concatenate([first, middle + pltpu.roll(cross, tail, 1), second], axis=1)

    def sweep(s, carry):
        now = lax.rem(s, 2)
        later = 1 - now
        for h in range(2 * reach):
            halo_out[now, h] = adj[now, halo_ref[h]]
        copies = [
            pltpu.make_async_remote_copy(
                halo_out.at[now, 0:reach],
                from_next.at[now],
                send_sem.at[now, 0],
                next_sem.at[now],
                device_id={"cell": before},
                device_id_type=MESH,
            ),
            pltpu.make_async_remote_copy(
                halo_out.at[now, reach : 2 * reach],
                from_prev.at[now],
                send_sem.at[now, 1],
                prev_sem.at[now],
                device_id={"cell": after},
                device_id_type=MESH,
            ),
        ]
        for g, (part, to, _, _) in enumerate(groups):
            copies.append(
                pltpu.make_async_remote_copy(
                    adj.at[now, part],
                    raw_in.at[now, part],
                    send_sem.at[now, 2 + g],
                    raw_sem.at[now, g],
                    device_id={"inst": to},
                    device_id_type=MESH,
                )
            )
        for copy in copies:
            copy.start()

        @pl.when(s == 0)
        def _():
            loads[4].wait()
            for r in range(rows):
                for t in range(2):
                    expand(t, r, 0, near.at[r, t])
                    for k in (1, 2):
                        expand(t, r, k, far.at[r, t, (k - 1) * wide : k * wide, :])

        for r in range(rows):
            x = split(adj[now, r])
            flux[r] = merge(
                join(jnp.dot(x[:, :wide], near[r, 0], preferred_element_type=jnp.float32)),
                join(jnp.dot(x[:, packed - wide :], near[r, 1], preferred_element_type=jnp.float32)),
            )

        for g, (part, _, to, x_first) in enumerate(groups):
            copies[2 + g].wait_recv()
            mine = choose(x_first, across, behind)
            theirs = choose(x_first, behind, ahead)
            for r in range(part.start, part.stop):
                part_out[now, r] = mix([(adj[now, r], mine), (raw_in[now, r], theirs)])
            copy = pltpu.make_async_remote_copy(
                part_out.at[now, part],
                part_in.at[now, part],
                send_sem.at[now, 4 + g],
                part_sem.at[now, g],
                device_id={"inst": to},
                device_id_type=MESH,
            )
            copy.start()
            copies.append(copy)
        for part, _, _, x_first in groups:
            theirs = choose(x_first, ahead, across)
            for r in range(part.start, part.stop):
                coupled[r] = mix([(adj[now, r], weights(0)), (raw_in[now, r], theirs)])

        copies[0].wait_recv()
        for h in range(reach):
            next_parts[h] = split(from_next[now, h])
        copies[1].wait_recv()
        for h in range(reach):
            prev_parts[h] = split(from_prev[now, h])
        for r in range(rows):
            p = prev_parts[jnp.clip(slots_ref[r, 1], 0, reach - 1)]
            q = next_parts[jnp.clip(slots_ref[r, 2] - reach - rows, 0, reach - 1)]
            flux[r] += merge(
                join(
                    jnp.dot(
                        jnp.concatenate([p[:, :wide], q[:, :wide]], axis=1),
                        far[r, 0],
                        preferred_element_type=jnp.float32,
                    )
                ),
                join(
                    jnp.dot(
                        jnp.concatenate([p[:, packed - wide :], q[:, packed - wide :]], axis=1),
                        far[r, 1],
                        preferred_element_type=jnp.float32,
                    )
                ),
            )

        for copy in copies[4:]:
            copy.wait_recv()
        for r in range(rows):
            old = adj[now, r]
            residual = live[r] * (src[r] - flux[r] - scale[r] * (coupled[r] + part_in[now, r]))
            new = old + step[r] * residual
            adj[later, r] = new

            @pl.when(s == ITERS - 1)
            def _():
                for out, value in ((adj_out, new), (res_out, residual)):
                    out[0, r, :, :main] = value[:, :main]
                    out[0, r, :, main:] = value[:, main:width]
                    out[1, r, :, :main] = value[:, wide:]
                    out[1, r, :, main:] = value[:, width:wide]

        for copy in copies:
            copy.wait_send()
        return carry

    lax.fori_loop(0, ITERS, sweep, 0)


def on_device(
    insts,
    cells,
    adjoint_init,
    source_term,
    jacobian,
    volume,
    pseudo_step,
    neighbor_slots,
    halo_blocks,
    padded_rows,
):
    inst_local, rows, objectives, width = adjoint_init.shape
    reach = halo_blocks.shape[0] // 2
    main = width // 128 * 128
    wide = main + 128
    packed = inst_local * width
    out = jax.ShapeDtypeStruct(adjoint_init.shape, jnp.float32)
    smem = pl.BlockSpec(memory_space=pltpu.SMEM)
    vmem = pl.BlockSpec(memory_space=pltpu.VMEM)
    f32, bf16 = jnp.float32, jnp.bfloat16
    block = (objectives, packed)
    parts = (objectives * TERMS, packed)
    flops = ITERS * 2 * rows * 3 * inst_local * 16 * width * width
    return pl.pallas_call(
        functools.partial(kernel, insts, cells),
        out_shape=(out, out),
        in_specs=[smem] * 3 + [pl.BlockSpec(memory_space=pltpu.HBM)] * 5,
        out_specs=(vmem, vmem),
        scratch_shapes=[
            pltpu.VMEM(adjoint_init.shape, f32),
            pltpu.VMEM(adjoint_init.shape, f32),
            pltpu.VMEM(jacobian.shape, bf16),
            pltpu.VMEM(volume.shape, f32),
            pltpu.VMEM(volume.shape, f32),
            pltpu.VMEM((2, rows) + block, f32),
            pltpu.VMEM((2, 2 * reach) + block, f32),
            pltpu.VMEM((2, reach) + block, f32),
            pltpu.VMEM((2, reach) + block, f32),
            pltpu.VMEM((2, rows) + block, f32),
            pltpu.VMEM((2, rows) + block, f32),
            pltpu.VMEM((2, rows) + block, f32),
            pltpu.VMEM((rows,) + block, f32),
            pltpu.VMEM((rows,) + block, f32),
            pltpu.VMEM((rows,) + block, f32),
            pltpu.VMEM((rows, 2, wide, wide), bf16),
            pltpu.VMEM((rows, 2, 2 * wide, wide), bf16),
            pltpu.VMEM((reach,) + parts, bf16),
            pltpu.VMEM((reach,) + parts, bf16),
            pltpu.VMEM((rows,) + block, f32),
            pltpu.VMEM((rows,) + block, f32),
            pltpu.SemaphoreType.DMA((2, 6)),
            pltpu.SemaphoreType.DMA((2,)),
            pltpu.SemaphoreType.DMA((2,)),
            pltpu.SemaphoreType.DMA((2, 2)),
            pltpu.SemaphoreType.DMA((2, 2)),
            pltpu.SemaphoreType.DMA((5,)),
        ],
        compiler_params=pltpu.CompilerParams(
            collective_id=0, has_side_effects=True, vmem_limit_bytes=40 * 1024 * 1024
        ),
        cost_estimate=pl.CostEstimate(
            flops=flops, bytes_accessed=2 * jacobian.size, transcendentals=0
        ),
        name="relax",
    )(
        neighbor_slots,
        halo_blocks,
        padded_rows,
        adjoint_init,
        source_term,
        jacobian,
        volume,
        pseudo_step,
    )


def solution(mesh):
    return jax.shard_map(
        functools.partial(on_device, mesh.shape["inst"], mesh.shape["cell"]),
        mesh=mesh,
        in_specs=(
            P("inst", "cell", None, None),
            P("inst", "cell", None, None),
            P("inst", "cell", None, None, None),
            P("cell", None),
            P("cell", None),
            P("cell", None),
            P("cell"),
            P("cell"),
        ),
        out_specs=(P("inst", "cell", None, None), P("inst", "cell", None, None)),
        check_vma=False,
    )
```

```python
import functools
import math

import jax
import jax.numpy as jnp
from jax import lax
from jax.experimental import pallas as pl
from jax.experimental.pallas import tpu as pltpu
from jax.sharding import PartitionSpec as P

ITERS = 16
TERMS = 2
MESH = pl.DeviceIdType.MESH

spectral_scale = 0.15


def time_weight(diff, count):
    diff = diff % count
    if diff == 0:
        return 0.0
    angle = math.pi * diff / count
    return 0.5 * (-1.0) ** diff * math.cos(angle) / math.sin(angle)


def kernel(
    insts,
    cells,
    slots_ref,
    halo_ref,
    pad_ref,
    init_hbm,
    src_hbm,
    jac_hbm,
    vol_hbm,
    step_hbm,
    adj_out,
    res_out,
    init_ref,
    src_in_ref,
    jac_ref,
    vol_ref,
    step_in_ref,
    adj,
    halo_out,
    halo_in,
    peers,
    src,
    step,
    scale,
    near,
    far,
    parts,
    flux,
    send_sem,
    halo_sem,
    peer_sem,
    load_sem,
):
    rows, width = vol_ref.shape
    reach = halo_in.shape[2]
    objectives = adj.shape[2]
    packed = adj.shape[3]
    main = width // 128 * 128
    tail = width - main
    wide = main + 128
    a = lax.axis_index("inst")
    d = lax.axis_index("cell")
    before = lax.rem(d + cells - 1, cells)
    after = lax.rem(d + 1, cells)
    others = [lax.rem(a + m, insts) for m in range(1, insts)]
    close = 1 - lax.rem(d, 2)
    sides = [close, 1 - close]
    neighbour = [before + side * (after - before) for side in sides]

    loads = [
        pltpu.make_async_copy(hbm, ref, load_sem.at[n])
        for n, (hbm, ref) in enumerate(
            (
                (init_hbm, init_ref),
                (src_hbm, src_in_ref),
                (vol_hbm, vol_ref),
                (step_hbm, step_in_ref),
                (jac_hbm, jac_ref),
            )
        )
    ]
    for load in loads:
        load.start()

    barrier = pltpu.get_barrier_semaphore()
    for c in (before, after):
        pl.semaphore_signal(barrier, inc=1, device_id={"cell": c}, device_id_type=MESH)
    for b in others:
        pl.semaphore_signal(barrier, inc=1, device_id={"inst": b}, device_id_type=MESH)

    def pack(first, second):
        return jnp.concatenate(
            [first[:, :main], first[:, main:], second[:, main:], second[:, :main]], axis=1
        )

    for load in loads[:4]:
        load.wait()
    for r in range(rows):
        adj[0, r] = pack(init_ref[0, r], init_ref[1, r])
        src[r] = pack(src_in_ref[0, r], src_in_ref[1, r])
        v = jnp.broadcast_to(vol_ref[r : r + 1, :], (objectives, width)) * spectral_scale
        scale[r] = pack(v, v)
        v = jnp.broadcast_to(step_in_ref[r : r + 1, :], (objectives, width))
        step[r] = pack(v, v)

    def expand(t, r, k, dst):
        block = jac_ref.at[t, r, k]
        if t == 0:
            dst[:width, :main] = block[:, :main]
            dst[:width, main:] = jnp.concatenate(
                [block[:, main:], jnp.zeros((width, 128 - tail), jnp.bfloat16)], axis=1
            )
            dst[width:, :] = jnp.zeros((wide - width, wide), jnp.bfloat16)
        else:
            for lo, hi, at in ((0, main, 128), (main, width, 128 - tail)):
                dst[at : at + hi - lo, 128:] = block[lo:hi, :main]
                dst[at : at + hi - lo, :128] = jnp.concatenate(
                    [jnp.zeros((hi - lo, 128 - tail), jnp.bfloat16), block[lo:hi, main:]], axis=1
                )
            dst[: 128 - tail, :] = jnp.zeros((128 - tail, wide), jnp.bfloat16)

    def split(x):
        parts = []
        for _ in range(TERMS):
            high = x.astype(jnp.bfloat16).astype(jnp.float32)
            parts.append(high)
            x = x - high
        return jnp.concatenate(parts, axis=0).astype(jnp.bfloat16)

    def join(x):
        total = x[objectives * (TERMS - 1) :]
        for n in reversed(range(TERMS - 1)):
            total = total + x[objectives * n : objectives * (n + 1)]
        return total

    def merge(first, second):
        return jnp.concatenate(
            [first[:, :main], first[:, main:] + second[:, :128], second[:, 128:]], axis=1
        )

    live = [
        jnp.where(r < rows - pad_ref[0], jnp.float32(1), jnp.float32(0)) for r in range(rows)
    ]
    lane = lax.broadcasted_iota(jnp.int32, (objectives, 128), 1)
    first_half = lane < tail

    pl.semaphore_wait(barrier, insts + 1)

    count = 2 * insts

    def weights(offset):
        return [time_weight(2 * offset + n, count) for n in (0, 1, -1)]

    def mix(sources):
        first, middle, second, cross = 0.0, 0.0, 0.0, 0.0
        for u, (same, up, down) in sources:
            u0, ut, u1 = u[:, :main], u[:, main:wide], u[:, wide:]
            first = first + same * u0 + up * u1
            second = second + same * u1 + down * u0
            middle = middle + same * ut
            cross = cross + jnp.where(first_half, down, up) * ut
        return jnp.concatenate([first, middle + pltpu.roll(cross, tail, 1), second], axis=1)

    def exchange(now):
        copies = []
        for n in range(2):
            copies.append(
                pltpu.make_async_remote_copy(
                    halo_out.at[now, sides[n]],
                    halo_in.at[now, 1 - sides[n]],
                    send_sem.at[now, n],
                    halo_sem.at[now, 1 - sides[n]],
                    device_id={"cell": neighbour[n]},
                    device_id_type=MESH,
                )
            )
        for m in range(1, insts):
            copies.append(
                pltpu.make_async_remote_copy(
                    adj.at[now],
                    peers.at[now, insts - m - 1],
                    send_sem.at[now, 1 + m],
                    peer_sem.at[now, insts - m - 1],
                    device_id={"inst": others[m - 1]},
                    device_id_type=MESH,
                )
            )
        return copies

    def arrival(now, n):
        return pltpu.make_async_remote_copy(
            halo_out.at[now, sides[n]],
            halo_in.at[now, sides[n]],
            send_sem.at[now, n],
            halo_sem.at[now, sides[n]],
            device_id={"cell": neighbour[n]},
            device_id_type=MESH,
        )

    def sweep(s, carry):
        now = lax.rem(s, 2)
        later = 1 - now
        for h in range(2 * reach):
            halo_out[now, h // reach, h % reach] = adj[now, halo_ref[h]]
        copies = exchange(now)
        for n in [1, 0] + [m for m in (3, 2, 4) if m <= insts] + list(range(5, insts + 1)):
            copies[n].start()

        @pl.when(s == 0)
        def _():
            loads[4].wait()
            for r in range(rows):
                for t in range(2):
                    expand(t, r, 0, near.at[r, t])
                    for k in (1, 2):
                        expand(t, r, k, far.at[k - 1, r, t])

        for r in range(rows):
            x = split(adj[now, r])
            flux[r] = merge(
                join(jnp.dot(x[:, :wide], near[r, 0], preferred_element_type=jnp.float32)),
                join(jnp.dot(x[:, packed - wide :], near[r, 1], preferred_element_type=jnp.float32)),
            )

        @pl.when(s > 0)
        def _():
            for copy in exchange(later):
                copy.wait_send()

        def incoming(n):
            side = sides[n]
            arrival(now, n).wait_recv()
            for h in range(reach):
                parts[h] = split(halo_in[now, side, h])
            for r in range(rows):
                code = slots_ref[r, 1 + side] - side * (reach + rows)
                x = parts[jnp.clip(code, 0, reach - 1)]
                yield merge(
                    join(jnp.dot(x[:, :wide], far[side, r, 0], preferred_element_type=jnp.float32)),
                    join(
                        jnp.dot(
                            x[:, packed - wide :],
                            far[side, r, 1],
                            preferred_element_type=jnp.float32,
                        )
                    ),
                )

        for r, value in enumerate(incoming(0)):
            flux[r] += value
        for copy in copies[2:]:
            copy.wait_recv()
        for r in range(rows):
            around = [(adj[now, r], weights(0))]
            around += [(peers[now, m - 1, r], weights(m)) for m in range(1, insts)]
            flux[r] = src[r] - flux[r] - scale[r] * mix(around)
        for r, value in enumerate(incoming(1)):
            old = adj[now, r]
            residual = live[r] * (flux[r] - value)
            new = old + step[r] * residual
            adj[later, r] = new

            @pl.when(s == ITERS - 1)
            def _():
                for out, value in ((adj_out, new), (res_out, residual)):
                    out[0, r, :, :main] = value[:, :main]
                    out[0, r, :, main:] = value[:, main:width]
                    out[1, r, :, :main] = value[:, wide:]
                    out[1, r, :, main:] = value[:, width:wide]

        return carry

    lax.fori_loop(0, ITERS, sweep, 0)
    for copy in exchange((ITERS - 1) % 2):
        copy.wait_send()


def on_device(
    insts,
    cells,
    adjoint_init,
    source_term,
    jacobian,
    volume,
    pseudo_step,
    neighbor_slots,
    halo_blocks,
    padded_rows,
):
    inst_local, rows, objectives, width = adjoint_init.shape
    reach = halo_blocks.shape[0] // 2
    main = width // 128 * 128
    wide = main + 128
    packed = inst_local * width
    out = jax.ShapeDtypeStruct(adjoint_init.shape, jnp.float32)
    smem = pl.BlockSpec(memory_space=pltpu.SMEM)
    vmem = pl.BlockSpec(memory_space=pltpu.VMEM)
    f32, bf16 = jnp.float32, jnp.bfloat16
    block = (objectives, packed)
    parts = (objectives * TERMS, packed)
    flops = ITERS * 2 * rows * 3 * inst_local * 16 * width * width
    return pl.pallas_call(
        functools.partial(kernel, insts, cells),
        out_shape=(out, out),
        in_specs=[smem] * 3 + [pl.BlockSpec(memory_space=pltpu.HBM)] * 5,
        out_specs=(vmem, vmem),
        scratch_shapes=[
            pltpu.VMEM(adjoint_init.shape, f32),
            pltpu.VMEM(adjoint_init.shape, f32),
            pltpu.VMEM(jacobian.shape, bf16),
            pltpu.VMEM(volume.shape, f32),
            pltpu.VMEM(volume.shape, f32),
            pltpu.VMEM((2, rows) + block, f32),
            pltpu.VMEM((2, 2, reach) + block, f32),
            pltpu.VMEM((2, 2, reach) + block, f32),
            pltpu.VMEM((2, insts - 1, rows) + block, f32),
            pltpu.VMEM((rows,) + block, f32),
            pltpu.VMEM((rows,) + block, f32),
            pltpu.VMEM((rows,) + block, f32),
            pltpu.VMEM((rows, 2, wide, wide), bf16),
            pltpu.VMEM((2, rows, 2, wide, wide), bf16),
            pltpu.VMEM((reach,) + parts, bf16),
            pltpu.VMEM((rows,) + block, f32),
            pltpu.SemaphoreType.DMA((2, insts + 1)),
            pltpu.SemaphoreType.DMA((2, 2)),
            pltpu.SemaphoreType.DMA((2, insts - 1)),
            pltpu.SemaphoreType.DMA((5,)),
        ],
        compiler_params=pltpu.CompilerParams(
            collective_id=0, has_side_effects=True, vmem_limit_bytes=40 * 1024 * 1024
        ),
        cost_estimate=pl.CostEstimate(
            flops=flops, bytes_accessed=2 * jacobian.size, transcendentals=0
        ),
        name="relax",
    )(
        neighbor_slots,
        halo_blocks,
        padded_rows,
        adjoint_init,
        source_term,
        jacobian,
        volume,
        pseudo_step,
    )


def solution(mesh):
    return jax.shard_map(
        functools.partial(on_device, mesh.shape["inst"], mesh.shape["cell"]),
        mesh=mesh,
        in_specs=(
            P("inst", "cell", None, None),
            P("inst", "cell", None, None),
            P("inst", "cell", None, None, None),
            P("cell", None),
            P("cell", None),
            P("cell", None),
            P("cell"),
            P("cell"),
        ),
        out_specs=(P("inst", "cell", None, None), P("inst", "cell", None, None)),
        check_vma=False,
    )
```

```python
import functools
import math

import jax
import jax.numpy as jnp
from jax import lax
from jax.experimental import pallas as pl
from jax.experimental.pallas import tpu as pltpu
from jax.sharding import PartitionSpec as P

ITERS = 16
TERMS = 2
MESH = pl.DeviceIdType.MESH

spectral_scale = 0.15


def time_weight(diff, count):
    diff = diff % count
    if diff == 0:
        return 0.0
    angle = math.pi * diff / count
    return 0.5 * (-1.0) ** diff * math.cos(angle) / math.sin(angle)


def kernel(
    insts,
    cells,
    slots_ref,
    halo_ref,
    pad_ref,
    init_hbm,
    src_hbm,
    jac_hbm,
    vol_hbm,
    step_hbm,
    adj_out,
    res_out,
    init_ref,
    src_in_ref,
    jac_ref,
    vol_ref,
    step_in_ref,
    adj,
    halo_out,
    from_prev,
    from_next,
    peers,
    src,
    step,
    scale,
    near,
    far,
    prev_parts,
    next_parts,
    flux,
    send_sem,
    prev_sem,
    next_sem,
    peer_sem,
    load_sem,
):
    rows, width = vol_ref.shape
    reach = from_prev.shape[1]
    objectives = adj.shape[2]
    packed = adj.shape[3]
    main = width // 128 * 128
    tail = width - main
    wide = main + 128
    a = lax.axis_index("inst")
    d = lax.axis_index("cell")
    before = lax.rem(d + cells - 1, cells)
    after = lax.rem(d + 1, cells)
    loads = [
        pltpu.make_async_copy(hbm, ref, load_sem.at[n])
        for n, (hbm, ref) in enumerate(
            (
                (init_hbm, init_ref),
                (src_hbm, src_in_ref),
                (vol_hbm, vol_ref),
                (step_hbm, step_in_ref),
                (jac_hbm, jac_ref),
            )
        )
    ]
    for load in loads:
        load.start()
    others = [lax.rem(a + m, insts) for m in range(1, insts)]

    barrier = pltpu.get_barrier_semaphore()
    for c in (before, after):
        pl.semaphore_signal(barrier, inc=1, device_id={"cell": c}, device_id_type=MESH)
    for b in others:
        pl.semaphore_signal(barrier, inc=1, device_id={"inst": b}, device_id_type=MESH)

    def pack(first, second):
        return jnp.concatenate(
            [first[:, :main], first[:, main:], second[:, main:], second[:, :main]], axis=1
        )

    for load in loads[:4]:
        load.wait()
    for r in range(rows):
        adj[0, r] = pack(init_ref[0, r], init_ref[1, r])
        src[r] = pack(src_in_ref[0, r], src_in_ref[1, r])
        v = jnp.broadcast_to(vol_ref[r : r + 1, :], (objectives, width)) * spectral_scale
        scale[r] = pack(v, v)
        v = jnp.broadcast_to(step_in_ref[r : r + 1, :], (objectives, width))
        step[r] = pack(v, v)

    def expand(t, r, k, dst):
        block = jac_ref.at[t, r, k]
        if t == 0:
            dst[:width, :main] = block[:, :main]
            dst[:width, main:] = jnp.concatenate(
                [block[:, main:], jnp.zeros((width, 128 - tail), jnp.bfloat16)], axis=1
            )
            dst[width:, :] = jnp.zeros((wide - width, wide), jnp.bfloat16)
        else:
            for lo, hi, at in ((0, main, 128), (main, width, 128 - tail)):
                dst[at : at + hi - lo, 128:] = block[lo:hi, :main]
                dst[at : at + hi - lo, :128] = jnp.concatenate(
                    [jnp.zeros((hi - lo, 128 - tail), jnp.bfloat16), block[lo:hi, main:]], axis=1
                )
            dst[: 128 - tail, :] = jnp.zeros((128 - tail, wide), jnp.bfloat16)

    def split(x):
        parts = []
        for _ in range(TERMS):
            high = x.astype(jnp.bfloat16).astype(jnp.float32)
            parts.append(high)
            x = x - high
        return jnp.concatenate(parts, axis=0).astype(jnp.bfloat16)

    def join(x):
        total = x[objectives * (TERMS - 1) :]
        for n in reversed(range(TERMS - 1)):
            total = total + x[objectives * n : objectives * (n + 1)]
        return total

    def merge(first, second):
        return jnp.concatenate(
            [first[:, :main], first[:, main:] + second[:, :128], second[:, 128:]], axis=1
        )

    live = [
        jnp.where(r < rows - pad_ref[0], jnp.float32(1), jnp.float32(0)) for r in range(rows)
    ]
    lane = lax.broadcasted_iota(jnp.int32, (objectives, 128), 1)
    first_half = lane < tail

    pl.semaphore_wait(barrier, insts + 1)

    def sweep(s, carry):
        now = lax.rem(s, 2)
        later = 1 - now
        for h in range(2 * reach):
            halo_out[now, h] = adj[now, halo_ref[h]]
        copies = [
            pltpu.make_async_remote_copy(
                halo_out.at[now, 0:reach],
                from_next.at[now],
                send_sem.at[now, 0],
                next_sem.at[now],
                device_id={"cell": before},
                device_id_type=MESH,
            ),
            pltpu.make_async_remote_copy(
                halo_out.at[now, reach : 2 * reach],
                from_prev.at[now],
                send_sem.at[now, 1],
                prev_sem.at[now],
                device_id={"cell": after},
                device_id_type=MESH,
            ),
        ]
        for m in range(1, insts):
            copies.append(
                pltpu.make_async_remote_copy(
                    adj.at[now],
                    peers.at[now, insts - m - 1],
                    send_sem.at[now, 1 + m],
                    peer_sem.at[now, insts - m - 1],
                    device_id={"inst": others[m - 1]},
                    device_id_type=MESH,
                )
            )
        for copy in copies:
            copy.start()

        @pl.when(s == 0)
        def _():
            loads[4].wait()
            for r in range(rows):
                for t in range(2):
                    expand(t, r, 0, near.at[r, t])
                    for k in (1, 2):
                        expand(t, r, k, far.at[r, t, (k - 1) * wide : k * wide, :])

        for r in range(rows):
            x = split(adj[now, r])
            flux[r] = merge(
                join(jnp.dot(x[:, :wide], near[r, 0], preferred_element_type=jnp.float32)),
                join(jnp.dot(x[:, packed - wide :], near[r, 1], preferred_element_type=jnp.float32)),
            )

        copies[0].wait_recv()
        for h in range(reach):
            next_parts[h] = split(from_next[now, h])
        copies[1].wait_recv()
        for h in range(reach):
            prev_parts[h] = split(from_prev[now, h])
        for r in range(rows):
            p = prev_parts[jnp.clip(slots_ref[r, 1], 0, reach - 1)]
            q = next_parts[jnp.clip(slots_ref[r, 2] - reach - rows, 0, reach - 1)]
            flux[r] += merge(
                join(
                    jnp.dot(
                        jnp.concatenate([p[:, :wide], q[:, :wide]], axis=1),
                        far[r, 0],
                        preferred_element_type=jnp.float32,
                    )
                ),
                join(
                    jnp.dot(
                        jnp.concatenate([p[:, packed - wide :], q[:, packed - wide :]], axis=1),
                        far[r, 1],
                        preferred_element_type=jnp.float32,
                    )
                ),
            )

        for copy in copies[2:]:
            copy.wait_recv()
        count = 2 * insts
        for r in range(rows):
            first, middle, second = 0.0, 0.0, 0.0
            cross = 0.0
            for m in range(insts):
                u = adj[now, r] if m == 0 else peers[now, m - 1, r]
                same = time_weight(2 * m, count)
                up = time_weight(2 * m + 1, count)
                down = time_weight(2 * m - 1, count)
                u0, ut, u1 = u[:, :main], u[:, main:wide], u[:, wide:]
                first = first + same * u0 + up * u1
                second = second + same * u1 + down * u0
                middle = middle + same * ut
                cross = cross + jnp.where(first_half, down, up) * ut
            middle = middle + pltpu.roll(cross, tail, 1)
            coupled = jnp.concatenate([first, middle, second], axis=1)
            old = adj[now, r]
            residual = live[r] * (src[r] - flux[r] - scale[r] * coupled)
            new = old + step[r] * residual
            adj[later, r] = new

            @pl.when(s == ITERS - 1)
            def _():
                for out, value in ((adj_out, new), (res_out, residual)):
                    out[0, r, :, :main] = value[:, :main]
                    out[0, r, :, main:] = value[:, main:width]
                    out[1, r, :, :main] = value[:, wide:]
                    out[1, r, :, main:] = value[:, width:wide]

        for copy in copies:
            copy.wait_send()
        return carry

    lax.fori_loop(0, ITERS, sweep, 0)


def on_device(
    insts,
    cells,
    adjoint_init,
    source_term,
    jacobian,
    volume,
    pseudo_step,
    neighbor_slots,
    halo_blocks,
    padded_rows,
):
    inst_local, rows, objectives, width = adjoint_init.shape
    reach = halo_blocks.shape[0] // 2
    main = width // 128 * 128
    wide = main + 128
    packed = inst_local * width
    out = jax.ShapeDtypeStruct(adjoint_init.shape, jnp.float32)
    smem = pl.BlockSpec(memory_space=pltpu.SMEM)
    vmem = pl.BlockSpec(memory_space=pltpu.VMEM)
    f32, bf16 = jnp.float32, jnp.bfloat16
    block = (objectives, packed)
    parts = (objectives * TERMS, packed)
    flops = ITERS * 2 * rows * 3 * inst_local * 16 * width * width
    return pl.pallas_call(
        functools.partial(kernel, insts, cells),
        out_shape=(out, out),
        in_specs=[smem] * 3 + [pl.BlockSpec(memory_space=pltpu.HBM)] * 5,
        out_specs=(vmem, vmem),
        scratch_shapes=[
            pltpu.VMEM(adjoint_init.shape, f32),
            pltpu.VMEM(adjoint_init.shape, f32),
            pltpu.VMEM(jacobian.shape, bf16),
            pltpu.VMEM(volume.shape, f32),
            pltpu.VMEM(volume.shape, f32),
            pltpu.VMEM((2, rows) + block, f32),
            pltpu.VMEM((2, 2 * reach) + block, f32),
            pltpu.VMEM((2, reach) + block, f32),
            pltpu.VMEM((2, reach) + block, f32),
            pltpu.VMEM((2, insts - 1, rows) + block, f32),
            pltpu.VMEM((rows,) + block, f32),
            pltpu.VMEM((rows,) + block, f32),
            pltpu.VMEM((rows,) + block, f32),
            pltpu.VMEM((rows, 2, wide, wide), bf16),
            pltpu.VMEM((rows, 2, 2 * wide, wide), bf16),
            pltpu.VMEM((reach,) + parts, bf16),
            pltpu.VMEM((reach,) + parts, bf16),
            pltpu.VMEM((rows,) + block, f32),
            pltpu.SemaphoreType.DMA((2, insts + 1)),
            pltpu.SemaphoreType.DMA((2,)),
            pltpu.SemaphoreType.DMA((2,)),
            pltpu.SemaphoreType.DMA((2, insts - 1)),
            pltpu.SemaphoreType.DMA((5,)),
        ],
        compiler_params=pltpu.CompilerParams(
            collective_id=0, has_side_effects=True, vmem_limit_bytes=64 * 1024 * 1024 - 256 * 1024
        ),
        cost_estimate=pl.CostEstimate(
            flops=flops, bytes_accessed=2 * jacobian.size, transcendentals=0
        ),
        name="relax",
    )(
        neighbor_slots,
        halo_blocks,
        padded_rows,
        adjoint_init,
        source_term,
        jacobian,
        volume,
        pseudo_step,
    )


def solution(mesh):
    return jax.shard_map(
        functools.partial(on_device, mesh.shape["inst"], mesh.shape["cell"]),
        mesh=mesh,
        in_specs=(
            P("inst", "cell", None, None),
            P("inst", "cell", None, None),
            P("inst", "cell", None, None, None),
            P("cell", None),
            P("cell", None),
            P("cell", None),
            P("cell"),
            P("cell"),
        ),
        out_specs=(P("inst", "cell", None, None), P("inst", "cell", None, None)),
        check_vma=False,
    )
```

```python
import functools
import math

import jax
import jax.numpy as jnp
from jax import lax
from jax.experimental import pallas as pl
from jax.experimental.pallas import tpu as pltpu
from jax.sharding import PartitionSpec as P

ITERS = 16
TERMS = 2
MESH = pl.DeviceIdType.MESH

spectral_scale = 0.15


def time_weight(diff, count):
    diff = diff % count
    if diff == 0:
        return 0.0
    angle = math.pi * diff / count
    return 0.5 * (-1.0) ** diff * math.cos(angle) / math.sin(angle)


def kernel(
    insts,
    cells,
    slots_ref,
    halo_ref,
    pad_ref,
    init_hbm,
    src_hbm,
    jac_hbm,
    vol_hbm,
    step_hbm,
    adj_out,
    res_out,
    init_ref,
    src_in_ref,
    jac_ref,
    vol_ref,
    step_in_ref,
    adj,
    halo_out,
    from_prev,
    from_next,
    peers,
    src,
    step,
    scale,
    near,
    far,
    prev_parts,
    next_parts,
    flux,
    send_sem,
    prev_sem,
    next_sem,
    peer_sem,
    load_sem,
):
    rows, width = vol_ref.shape
    reach = from_prev.shape[1]
    objectives = adj.shape[2]
    packed = adj.shape[3]
    main = width // 128 * 128
    tail = width - main
    wide = main + 128
    a = lax.axis_index("inst")
    d = lax.axis_index("cell")
    before = lax.rem(d + cells - 1, cells)
    after = lax.rem(d + 1, cells)
    loads = [
        pltpu.make_async_copy(hbm, ref, load_sem.at[n])
        for n, (hbm, ref) in enumerate(
            (
                (init_hbm, init_ref),
                (src_hbm, src_in_ref),
                (vol_hbm, vol_ref),
                (step_hbm, step_in_ref),
                (jac_hbm, jac_ref),
            )
        )
    ]
    for load in loads:
        load.start()
    others = [lax.rem(a + m, insts) for m in range(1, insts)]

    barrier = pltpu.get_barrier_semaphore()
    for c in (before, after):
        pl.semaphore_signal(barrier, inc=1, device_id={"cell": c}, device_id_type=MESH)
    for b in others:
        pl.semaphore_signal(barrier, inc=1, device_id={"inst": b}, device_id_type=MESH)

    def pack(first, second):
        return jnp.concatenate(
            [first[:, :main], first[:, main:], second[:, main:], second[:, :main]], axis=1
        )

    for load in loads[:4]:
        load.wait()
    for r in range(rows):
        adj[0, r] = pack(init_ref[0, r], init_ref[1, r])
        src[r] = pack(src_in_ref[0, r], src_in_ref[1, r])
        v = jnp.broadcast_to(vol_ref[r : r + 1, :], (objectives, width)) * spectral_scale
        scale[r] = pack(v, v)
        v = jnp.broadcast_to(step_in_ref[r : r + 1, :], (objectives, width))
        step[r] = pack(v, v)

    def expand(t, r, k, dst):
        block = jac_ref.at[t, r, k]
        if t == 0:
            dst[:width, :main] = block[:, :main]
            dst[:width, main:] = jnp.concatenate(
                [block[:, main:], jnp.zeros((width, 128 - tail), jnp.bfloat16)], axis=1
            )
            dst[width:, :] = jnp.zeros((wide - width, wide), jnp.bfloat16)
        else:
            for lo, hi, at in ((0, main, 128), (main, width, 128 - tail)):
                dst[at : at + hi - lo, 128:] = block[lo:hi, :main]
                dst[at : at + hi - lo, :128] = jnp.concatenate(
                    [jnp.zeros((hi - lo, 128 - tail), jnp.bfloat16), block[lo:hi, main:]], axis=1
                )
            dst[: 128 - tail, :] = jnp.zeros((128 - tail, wide), jnp.bfloat16)

    def split(x):
        parts = []
        for _ in range(TERMS):
            high = x.astype(jnp.bfloat16).astype(jnp.float32)
            parts.append(high)
            x = x - high
        return jnp.concatenate(parts, axis=0).astype(jnp.bfloat16)

    def join(x):
        total = x[objectives * (TERMS - 1) :]
        for n in reversed(range(TERMS - 1)):
            total = total + x[objectives * n : objectives * (n + 1)]
        return total

    def merge(first, second):
        return jnp.concatenate(
            [first[:, :main], first[:, main:] + second[:, :128], second[:, 128:]], axis=1
        )

    live = [
        jnp.where(r < rows - pad_ref[0], jnp.float32(1), jnp.float32(0)) for r in range(rows)
    ]
    lane = lax.broadcasted_iota(jnp.int32, (objectives, 128), 1)
    first_half = lane < tail

    pl.semaphore_wait(barrier, insts + 1)

    def exchange(now):
        copies = [
            pltpu.make_async_remote_copy(
                halo_out.at[now, 0:reach],
                from_next.at[now],
                send_sem.at[now, 0],
                next_sem.at[now],
                device_id={"cell": before},
                device_id_type=MESH,
            ),
            pltpu.make_async_remote_copy(
                halo_out.at[now, reach : 2 * reach],
                from_prev.at[now],
                send_sem.at[now, 1],
                prev_sem.at[now],
                device_id={"cell": after},
                device_id_type=MESH,
            ),
        ]
        for m in range(1, insts):
            copies.append(
                pltpu.make_async_remote_copy(
                    adj.at[now],
                    peers.at[now, insts - m - 1],
                    send_sem.at[now, 1 + m],
                    peer_sem.at[now, insts - m - 1],
                    device_id={"inst": others[m - 1]},
                    device_id_type=MESH,
                )
            )
        return copies

    def sweep(s, carry):
        now = lax.rem(s, 2)
        later = 1 - now
        for h in range(2 * reach):
            halo_out[now, h] = adj[now, halo_ref[h]]
        copies = exchange(now)
        for copy in copies:
            copy.start()

        @pl.when(s == 0)
        def _():
            loads[4].wait()
            for r in range(rows):
                for t in range(2):
                    expand(t, r, 0, near.at[r, t])
                    for k in (1, 2):
                        expand(t, r, k, far.at[r, t, (k - 1) * wide : k * wide, :])

        for r in range(rows):
            x = split(adj[now, r])
            flux[r] = merge(
                join(jnp.dot(x[:, :wide], near[r, 0], preferred_element_type=jnp.float32)),
                join(jnp.dot(x[:, packed - wide :], near[r, 1], preferred_element_type=jnp.float32)),
            )

        @pl.when(s > 0)
        def _():
            for copy in exchange(later):
                copy.wait_send()

        copies[0].wait_recv()
        for h in range(reach):
            next_parts[h] = split(from_next[now, h])
        copies[1].wait_recv()
        for h in range(reach):
            prev_parts[h] = split(from_prev[now, h])
        for r in range(rows):
            p = prev_parts[jnp.clip(slots_ref[r, 1], 0, reach - 1)]
            q = next_parts[jnp.clip(slots_ref[r, 2] - reach - rows, 0, reach - 1)]
            flux[r] += merge(
                join(
                    jnp.dot(
                        jnp.concatenate([p[:, :wide], q[:, :wide]], axis=1),
                        far[r, 0],
                        preferred_element_type=jnp.float32,
                    )
                ),
                join(
                    jnp.dot(
                        jnp.concatenate([p[:, packed - wide :], q[:, packed - wide :]], axis=1),
                        far[r, 1],
                        preferred_element_type=jnp.float32,
                    )
                ),
            )

        for copy in copies[2:]:
            copy.wait_recv()
        count = 2 * insts
        for r in range(rows):
            first, middle, second = 0.0, 0.0, 0.0
            cross = 0.0
            for m in range(insts):
                u = adj[now, r] if m == 0 else peers[now, m - 1, r]
                same = time_weight(2 * m, count)
                up = time_weight(2 * m + 1, count)
                down = time_weight(2 * m - 1, count)
                u0, ut, u1 = u[:, :main], u[:, main:wide], u[:, wide:]
                first = first + same * u0 + up * u1
                second = second + same * u1 + down * u0
                middle = middle + same * ut
                cross = cross + jnp.where(first_half, down, up) * ut
            middle = middle + pltpu.roll(cross, tail, 1)
            coupled = jnp.concatenate([first, middle, second], axis=1)
            old = adj[now, r]
            residual = live[r] * (src[r] - flux[r] - scale[r] * coupled)
            new = old + step[r] * residual
            adj[later, r] = new

            @pl.when(s == ITERS - 1)
            def _():
                for out, value in ((adj_out, new), (res_out, residual)):
                    out[0, r, :, :main] = value[:, :main]
                    out[0, r, :, main:] = value[:, main:width]
                    out[1, r, :, :main] = value[:, wide:]
                    out[1, r, :, main:] = value[:, width:wide]

        return carry

    lax.fori_loop(0, ITERS, sweep, 0)
    for copy in exchange((ITERS - 1) % 2):
        copy.wait_send()


def on_device(
    insts,
    cells,
    adjoint_init,
    source_term,
    jacobian,
    volume,
    pseudo_step,
    neighbor_slots,
    halo_blocks,
    padded_rows,
):
    inst_local, rows, objectives, width = adjoint_init.shape
    reach = halo_blocks.shape[0] // 2
    main = width // 128 * 128
    wide = main + 128
    packed = inst_local * width
    out = jax.ShapeDtypeStruct(adjoint_init.shape, jnp.float32)
    smem = pl.BlockSpec(memory_space=pltpu.SMEM)
    vmem = pl.BlockSpec(memory_space=pltpu.VMEM)
    f32, bf16 = jnp.float32, jnp.bfloat16
    block = (objectives, packed)
    parts = (objectives * TERMS, packed)
    flops = ITERS * 2 * rows * 3 * inst_local * 16 * width * width
    return pl.pallas_call(
        functools.partial(kernel, insts, cells),
        out_shape=(out, out),
        in_specs=[smem] * 3 + [pl.BlockSpec(memory_space=pltpu.HBM)] * 5,
        out_specs=(vmem, vmem),
        scratch_shapes=[
            pltpu.VMEM(adjoint_init.shape, f32),
            pltpu.VMEM(adjoint_init.shape, f32),
            pltpu.VMEM(jacobian.shape, bf16),
            pltpu.VMEM(volume.shape, f32),
            pltpu.VMEM(volume.shape, f32),
            pltpu.VMEM((2, rows) + block, f32),
            pltpu.VMEM((2, 2 * reach) + block, f32),
            pltpu.VMEM((2, reach) + block, f32),
            pltpu.VMEM((2, reach) + block, f32),
            pltpu.VMEM((2, insts - 1, rows) + block, f32),
            pltpu.VMEM((rows,) + block, f32),
            pltpu.VMEM((rows,) + block, f32),
            pltpu.VMEM((rows,) + block, f32),
            pltpu.VMEM((rows, 2, wide, wide), bf16),
            pltpu.VMEM((rows, 2, 2 * wide, wide), bf16),
            pltpu.VMEM((reach,) + parts, bf16),
            pltpu.VMEM((reach,) + parts, bf16),
            pltpu.VMEM((rows,) + block, f32),
            pltpu.SemaphoreType.DMA((2, insts + 1)),
            pltpu.SemaphoreType.DMA((2,)),
            pltpu.SemaphoreType.DMA((2,)),
            pltpu.SemaphoreType.DMA((2, insts - 1)),
            pltpu.SemaphoreType.DMA((5,)),
        ],
        compiler_params=pltpu.CompilerParams(
            collective_id=0, has_side_effects=True, vmem_limit_bytes=64 * 1024 * 1024 - 512 * 1024
        ),
        cost_estimate=pl.CostEstimate(
            flops=flops, bytes_accessed=2 * jacobian.size, transcendentals=0
        ),
        name="relax",
    )(
        neighbor_slots,
        halo_blocks,
        padded_rows,
        adjoint_init,
        source_term,
        jacobian,
        volume,
        pseudo_step,
    )


def solution(mesh):
    return jax.shard_map(
        functools.partial(on_device, mesh.shape["inst"], mesh.shape["cell"]),
        mesh=mesh,
        in_specs=(
            P("inst", "cell", None, None),
            P("inst", "cell", None, None),
            P("inst", "cell", None, None, None),
            P("cell", None),
            P("cell", None),
            P("cell", None),
            P("cell"),
            P("cell"),
        ),
        out_specs=(P("inst", "cell", None, None), P("inst", "cell", None, None)),
        check_vma=False,
    )
```
